256 devices in a mesh: context: 64 (over z, x, y_hi), tensor: 4 (over y_lo, core).
Axes of the slice: x: 4, y: 4 (y_hi: 2, y_lo: 2; y = y_hi * 2 + y_lo), z: 8, core: 2. Of those that a mesh axis runs over, the one named last changes fastest.
Arguments:
- queries: bfloat16 [256, 128, 128], P('tensor'), may hold values from -18 to 18
- prompt_keys: bfloat16 [256, 8, 128], P('tensor'), may hold values from -6 to 6
- prompt_values: bfloat16 [256, 8, 128], P('tensor'), may hold values from -6 to 6
- cache_keys: bfloat16 [131072, 8, 128], P('context', 'tensor'), may hold values from -6 to 6
- cache_values: bfloat16 [131072, 8, 128], P('context', 'tensor'), may hold values from -6 to 6
- cache_lengths: int32 [64], P('context'), may hold values from 1 to 2048, 98304 in all
- offset: int32 [1], replicated, may hold values from 1 to 32767
- prompt_positions: int32 [256], P('tensor'), may hold values from 0 to 510, as said below
Outputs:
- attended: bfloat16 [256, 128, 128], P('context', 'tensor')
The draws below stay inside these ranges and needn't reach their ends.
Inputs may be any that keep to these rules, and one draw needn't show every extreme that they name: `cache_lengths`: they sum to three quarters of 131072. `prompt_positions`: strictly increasing from 0 to 510, steps of 1 to 3.
All inputs are finite; a program needn't handle non-finite values. No bound on the sum of `cache_lengths` on one device may be relied on, other than what follows from the above.
Results may differ from the reference program's by a relative error of at most 0.0095.
The reference program's roundings to bfloat16 on the way count: a program that leaves them out, or rounds other values in their place, can miss the bound.
Values may be sent and summed in bfloat16 or wider, within the bound.
No kernel may reach another device: no remote copies, remote signals or barrier semaphores. Data moves between devices by JAX's collectives and lax.ppermute only.
A program may use at most 128 MiB of HBM per device.

```python
import math
import jax
import jax.numpy as jnp
import numpy as np
from jax import lax

Q_HEADS = 128
KV_HEADS = 8
HEAD_DIM = 128
CACHE_DEV = 2048
PROMPT = 256
Q_DEV = 4
CACHE = 131072
N_CONTEXT = 64


def draw_queries(key, part):
    key = jax.random.fold_in(key, 11)
    base_key = jax.random.fold_in(key, 0)
    base = jnp.clip(jax.random.normal(base_key, (PROMPT, Q_HEADS, HEAD_DIM), jnp.float32), -6.0, 6.0)
    return base.astype(jnp.bfloat16)


def draw_prompt_keys(key, part):
    key = jax.random.fold_in(key, 23)
    base = jnp.clip(jax.random.normal(key, (PROMPT, KV_HEADS, HEAD_DIM), jnp.float32), -6.0, 6.0)
    return base.astype(jnp.bfloat16)


def draw_prompt_positions(key, part):
    key = jax.random.fold_in(key, 37)
    rows = jnp.arange(PROMPT, dtype=jnp.int32)
    dropped = jax.random.randint(key, (PROMPT,), 0, 2, jnp.int32)
    dropped = jnp.where((rows == 0) | (rows == PROMPT - 1), 0, dropped)
    return (2 * rows - dropped).astype(jnp.int32)


def shard_levels(own_key, shape, pieces, least, largest):
    factor_of, own = 1.0, jax.random.fold_in(own_key, 6)
    for dim, blocks in pieces:
        draws = jnp.exp(jax.random.uniform(jax.random.fold_in(own, dim), (blocks,), jnp.float32, least / len(pieces), largest / len(pieces)))
        factor_of = factor_of * jnp.repeat(draws, shape[dim] // blocks).reshape([-1 if axis == dim else 1 for axis in range(len(shape))])
    return factor_of


def length_profile(amount, total, reach, skew):
    weights = [(1 << 20) // math.isqrt(grade ** skew) + 1 for grade in range(2, amount + 1)]
    rest, given = total - reach - (amount - 1), [1] * (amount - 1)
    while rest > 0:
        free = [i for i in range(amount - 1) if given[i] < reach]
        pool, left = sum([weights[i] for i in free]), rest
        for i in free:
            extra = min(reach - given[i], max(1, left * weights[i] // pool), rest)
            given[i] = given[i] + extra
            rest = rest - extra
    return np.array([reach] + given)


def ragged_sizes(stream_key, amount, total, bound, lean):
    if amount == 2:
        one = jax.random.randint(stream_key, (), max(1, total - bound), min(bound, total - 1) + 1)
        return jnp.stack([one, total - one])
    lengths = jnp.asarray(length_profile(amount, total, bound, lean), jnp.int32)
    twos = (amount - 1) // 2
    giver, taker = lengths[1:1 + 2 * twos:2], lengths[2:2 + 2 * twos:2]
    room = jnp.minimum(giver - 1, bound - taker)
    shifted = jax.random.randint(jax.random.fold_in(stream_key, 1), (twos,), 0, 1 << 20) % (room + 1)
    lengths = lengths.at[1:1 + 2 * twos:2].set(giver - shifted).at[2:2 + 2 * twos:2].set(taker + shifted)
    return lengths[jax.random.permutation(jax.random.fold_in(stream_key, 2), amount)]


def centred(stream_key, dims, deviation, most, pieces=(), kind=jnp.bfloat16):
    result = jax.random.normal(stream_key, dims, jnp.float32) * deviation
    if len(pieces) > 0:
        result = shard_levels(stream_key, dims, pieces, -0.22, 0.18) * result
    return jnp.clip(result, min=-most, max=most).astype(kind)


def setup_inputs(seed: int = 0) -> dict:
    streams_of = jax.random.split(jax.random.key(seed), 9)
    queries = draw_queries(jax.random.fold_in(streams_of[8], 71), 0)
    prompt_keys = draw_prompt_keys(jax.random.fold_in(streams_of[8], 71), 0)
    prompt_values = centred(streams_of[2], (PROMPT, KV_HEADS, HEAD_DIM), 1.0, 6.0, ((0, 4),))
    cache_keys = centred(streams_of[3], (CACHE, KV_HEADS, HEAD_DIM), 1.0, 6.0, ((0, 64), (1, 4)))
    cache_values = centred(streams_of[4], (CACHE, KV_HEADS, HEAD_DIM), 1.0, 6.0, ((0, 64), (1, 4)))
    cache_lengths = ragged_sizes(streams_of[5], N_CONTEXT, N_CONTEXT * CACHE_DEV * 3 // 4, CACHE_DEV, 1).astype(jnp.int32)
    offset = jax.random.randint(streams_of[6], (1,), 1, 32768).astype(jnp.int32)
    prompt_positions = draw_prompt_positions(jax.random.fold_in(streams_of[8], 71), 0)
    return dict(queries=queries, prompt_keys=prompt_keys, prompt_values=prompt_values, cache_keys=cache_keys, cache_values=cache_values, cache_lengths=cache_lengths, offset=offset, prompt_positions=prompt_positions)


def rotate(values, position):
    width = values.shape[-1]
    half = width // 2
    freq = jnp.exp(jnp.arange(half, dtype=jnp.float32) * (-2.0 * math.log(500000.0) / width))
    angle = position.astype(jnp.float32)[:, None] * freq[None, :]
    cosine = jnp.cos(angle)[:, None, :]
    sine = jnp.sin(angle)[:, None, :]
    wide = values.astype(jnp.float32)
    first = wide[..., :half]
    second = wide[..., half:]
    return jnp.concatenate([first * cosine - second * sine, second * cosine + first * sine], axis=-1)

def reference(queries, prompt_keys, prompt_values, cache_keys, cache_values, cache_lengths, offset, prompt_positions):
    position = offset[0] + prompt_positions
    turned_q = rotate(queries, position).astype(jnp.bfloat16)
    turned_k = rotate(prompt_keys, position).astype(jnp.bfloat16)
    turned_q = lax.optimization_barrier(turned_q)
    turned_k = lax.optimization_barrier(turned_k)
    group = Q_HEADS // KV_HEADS
    scale = 1.0 / math.sqrt(HEAD_DIM)
    grouped = turned_q.astype(jnp.float32).reshape(PROMPT, KV_HEADS, group, HEAD_DIM)
    shard_keys = cache_keys.reshape(N_CONTEXT, CACHE_DEV, KV_HEADS, HEAD_DIM)
    shard_vals = cache_values.reshape(N_CONTEXT, CACHE_DEV, KV_HEADS, HEAD_DIM)
    block_keys = turned_k.reshape(N_CONTEXT, Q_DEV, KV_HEADS, HEAD_DIM)
    block_vals = prompt_values.reshape(N_CONTEXT, Q_DEV, KV_HEADS, HEAD_DIM)
    query_rows = jnp.arange(PROMPT, dtype=jnp.int32)
    indices = jnp.arange(N_CONTEXT, dtype=jnp.int32)

    def shard(carry, items):
        best, numer, denom = carry
        keys, vals, pkeys, pvals, length, index = items
        cache_scores = jnp.einsum('rkgd,ckd->rkgc', grouped, keys.astype(jnp.float32)) * scale
        own_scores = jnp.einsum('rkgd,jkd->rkgj', grouped, pkeys.astype(jnp.float32)) * scale
        live = jnp.arange(CACHE_DEV, dtype=jnp.int32) < length
        key_rows = index * Q_DEV + jnp.arange(Q_DEV, dtype=jnp.int32)
        visible = (key_rows[None, :] <= query_rows[:, None])[:, None, None, :]
        cache_scores = jnp.where(live, cache_scores, -jnp.inf)
        own_scores = jnp.where(visible, own_scores, -jnp.inf)
        peak = jnp.maximum(cache_scores.max(-1), own_scores.max(-1))
        cache_weights = jnp.where(live, jnp.exp(cache_scores - peak[..., None]), 0.0).astype(jnp.bfloat16)
        own_weights = jnp.where(visible, jnp.exp(own_scores - peak[..., None]), 0.0).astype(jnp.bfloat16)
        cache_weights = lax.optimization_barrier(cache_weights).astype(jnp.float32)
        own_weights = lax.optimization_barrier(own_weights).astype(jnp.float32)
        total = cache_weights.sum(-1) + own_weights.sum(-1)
        output = jnp.einsum('rkgc,ckd->rkgd', cache_weights, vals.astype(jnp.float32))
        output = output + jnp.einsum('rkgj,jkd->rkgd', own_weights, pvals.astype(jnp.float32))
        new_best = jnp.maximum(best, peak)
        older = jnp.exp(best - new_best)
        newer = jnp.exp(peak - new_best)
        numer = numer * older[..., None] + output * newer[..., None]
        denom = denom * older + total * newer
        return ((new_best, numer, denom), None)
    start = (jnp.full((PROMPT, KV_HEADS, group), -jnp.inf, jnp.float32), jnp.zeros((PROMPT, KV_HEADS, group, HEAD_DIM), jnp.float32), jnp.zeros((PROMPT, KV_HEADS, group), jnp.float32))
    (best, numer, denom), unused = lax.scan(shard, start, (shard_keys, shard_vals, block_keys, block_vals, cache_lengths, indices))
    attended = numer / denom[..., None]
    return attended.reshape(PROMPT, Q_HEADS, HEAD_DIM).astype(jnp.bfloat16)
```

```python
import functools
import math

import jax
import jax.numpy as jnp
from jax import lax
from jax.experimental import pallas as pl
from jax.experimental.pallas import tpu as pltpu
from jax.sharding import PartitionSpec as P

SCALE = math.log2(math.e) / math.sqrt(128.0)
BF = jnp.bfloat16
F32 = jnp.float32
MIB = 2**20
KEY_BLOCK = 512
SUB = 256


def linear(z, x, y, core):
    y = y % 4
    return ((z % 8) * 8 + (x % 4) * 2 + y // 2) * 4 + (y % 2) * 2 + core % 2


def shift(dy, dcore):
    return [
        (linear(z, x, y, k), linear(z, x, y + dy, k + dcore))
        for z in range(8)
        for x in range(4)
        for y in range(4)
        for k in range(2)
    ]


def dot_nt(a, b):
    return lax.dot_general(a, b, (((1,), (1,)), ((), ())), preferred_element_type=F32)


def dot_nn(a, b):
    return jnp.dot(a, b, preferred_element_type=F32)


def turn_kernel(slots, cos_ref, sin_ref, *refs, with_kv):
    count = 16
    i = pl.program_id(0)
    ins, refs = refs[:4], refs[4:]
    kvs, outs = (refs[:4], refs[4:]) if with_kv else (None, refs)
    cosine = cos_ref[...][:, None, :]
    sine = sin_ref[...][:, None, :]
    start = pl.multiple_of(i * count * 16, count * 16)
    for j in range(4):
        wide = ins[j][...].astype(F32)
        flat = wide.reshape(count * 16, 128)
        turned = pltpu.roll(flat, 64, 1).reshape(count, 16, 128)
        value = (wide * cosine + turned * sine).astype(BF)
        outs[j][pl.ds(start, count * 16), :] = value.reshape(count * 16, 128)
    if with_kv:

        @pl.when(i == 0)
        def _():
            for j in range(4):
                outs[j][1024:1280, :] = kvs[j][...].reshape(256, 128)


def turn(queries, cosine, sine, kv, slots, head):
    with_kv = kv is not None
    rows = 1280 if with_kv else 1024

    def q_spec(j):
        return pl.BlockSpec((16, 16, 128), lambda i, s: (i, 2 * s[j] + head, 0))

    def kv_spec(j):
        return pl.BlockSpec((2, 2, 64, 128), lambda i, s: (s[j], 0, 0, 0))

    in_specs = [pl.BlockSpec((16, 128), lambda i, s: (i, 0))] * 2
    in_specs += [q_spec(j) for j in range(4)]
    args = [cosine, sine] + [queries] * 4
    if with_kv:
        in_specs += [kv_spec(j) for j in range(4)]
        args += [kv] * 4
    return pl.pallas_call(
        functools.partial(turn_kernel, with_kv=with_kv),
        grid_spec=pltpu.PrefetchScalarGridSpec(
            num_scalar_prefetch=1,
            grid=(4,),
            in_specs=in_specs,
            out_specs=[pl.BlockSpec((rows, 128), lambda i, s: (0, 0))] * 4,
        ),
        out_shape=[jax.ShapeDtypeStruct((rows, 128), BF)] * 4,
        compiler_params=pltpu.CompilerParams(vmem_limit_bytes=24 * MIB),
        name="turn%d" % head,
    )(slots, *args)


def eye_mask(rows):
    row = lax.broadcasted_iota(jnp.int32, (rows, 128), 0)
    lane = lax.broadcasted_iota(jnp.int32, (rows, 128), 1)
    return row, lane


def attend_kernel(slots, length, q0, q1, q2, q3, k_ref, v_ref, o_ref, q_s, k_s, v_s, st_s):
    j = pl.program_id(0)

    @pl.when(j == 0)
    def _():
        row = lax.broadcasted_iota(jnp.int32, (2048, 128), 0)
        live = row < length[0]
        first = k_ref[0:1, :].astype(F32)
        k_s[...] = jnp.where(live, k_ref[...].astype(F32), first).astype(BF)
        v_s[:, 0:128] = jnp.where(live, v_ref[...].astype(F32), 0.0).astype(BF)
        v_s[:, 128:256] = jnp.where(live, 1.0, 0.0).astype(BF)

    for n, ref in enumerate((q0, q1, q2, q3)):

        @pl.when(j == n)
        def _():
            q_s[...] = ref[...]

    slot = slots[j]
    row, lane = eye_mask(64)
    for s in range(4):
        q = q_s[s * SUB : (s + 1) * SUB, :]
        peak = None
        for b in range(2048 // KEY_BLOCK):
            keys = slice(b * KEY_BLOCK, (b + 1) * KEY_BLOCK)
            scores = dot_nt(q, k_s[keys, :])
            top = jnp.ceil(jnp.max(scores, axis=1, keepdims=True) * SCALE)
            new = top if peak is None else jnp.maximum(peak, top)
            weights = jnp.exp2(scores * SCALE - new).astype(BF)
            part = dot_nn(weights, v_s[keys, :])
            acc = part if peak is None else acc * jnp.exp2(peak - new) + part
            peak = new
        zrow = pl.multiple_of((2 * slot + s // 2) * 64, 64)
        for d in range(4):
            dest = 4 * (s % 2) + d
            rows = slice(d * 64, (d + 1) * 64)
            o_ref[dest, pl.ds(zrow, 64), :] = acc[rows, 0:128].astype(BF)
            pair = jnp.where(
                lane == row, peak[rows, :], jnp.where(lane == row + 64, acc[rows, 128:256], 0.0)
            )
            st_s[dest, pl.ds(2 * slot + s // 2, 1), :] = jnp.sum(pair, axis=0, keepdims=True)

    @pl.when(j == 3)
    def _():
        for dest in range(8):
            stats = st_s[dest]
            high = stats.astype(BF).astype(F32)
            o_ref[dest, 512:528, :] = jnp.concatenate([high, stats - high], axis=0).astype(BF)


def attend(qs, keys, values, slots, length, head):
    whole = lambda j, s, n: (0, 0)
    cache = pl.BlockSpec((None, 2048, 128), lambda j, s, n: (head, 0, 0))
    return pl.pallas_call(
        attend_kernel,
        grid_spec=pltpu.PrefetchScalarGridSpec(
            num_scalar_prefetch=2,
            grid=(4,),
            in_specs=[pl.BlockSpec((1024, 128), whole)] * 4 + [cache, cache],
            out_specs=pl.BlockSpec((8, 528, 128), lambda j, s, n: (0, 0, 0)),
            scratch_shapes=[
                pltpu.VMEM((1024, 128), BF),
                pltpu.VMEM((2048, 128), BF),
                pltpu.VMEM((2048, 256), BF),
                pltpu.VMEM((8, 8, 128), F32),
            ],
        ),
        out_shape=jax.ShapeDtypeStruct((8, 528, 128), BF),
        compiler_params=pltpu.CompilerParams(vmem_limit_bytes=40 * MIB),
        cost_estimate=pl.CostEstimate(
            flops=4 * 4096 * 2048 * 128, bytes_accessed=4 * MIB, transcendentals=4096 * 2048
        ),
        name="attend%d" % head,
    )(slots, length, *qs, keys, values)


def weigh(stats):
    peak = functools.reduce(jnp.maximum, stats)
    factors = [jnp.exp2(s - peak) for s in stats]
    sums = [pltpu.roll(s, 64, 1) for s in stats]
    return peak, factors, sums


def spread(pairs, row, lane):
    hit = (lane == row) | (lane == row + 64)
    return jnp.concatenate([jnp.where(hit, p, 0.0) for p in pairs], axis=1)


def pair_up(first, second, lane):
    return jnp.where(lane[0:1] < 64, first, pltpu.roll(second, 64, 1))


def fold_kernel(a_ref, b_ref, o_ref):
    row, lane = eye_mask(64)
    lane8 = lax.broadcasted_iota(jnp.int32, (8, 128), 1)
    tile = lax.broadcasted_iota(jnp.int32, (16, 128), 0)
    news = []
    for h, ref in enumerate((a_ref, b_ref)):
        stats = []
        for src in range(8):
            block = ref[src, 512:528, :].astype(F32)
            stats.append(block[0:8] + block[8:16])
        peak, factors, sums = weigh(stats)
        factors = [f.astype(BF).astype(F32) for f in factors]
        total = functools.reduce(jnp.add, [f * s for f, s in zip(factors, sums)])
        rolled = [pltpu.roll(f, 64, 1) for f in factors]
        joined = [jnp.where(lane8 < 64, factors[2 * p], rolled[2 * p + 1]) for p in range(4)]
        for z in range(8):
            mix = spread([x[z : z + 1] for x in joined], row, lane).astype(BF)
            parts = ref[:, z * 64 : z * 64 + 64, :].reshape(512, 128)
            o_ref[z, h * 64 : h * 64 + 64, :] = dot_nn(mix, parts).astype(BF)
        new = jnp.where(lane8 < 64, peak, pltpu.roll(total, 64, 1))
        high = new.astype(BF).astype(F32)
        news += [high, new - high]
    for z in range(8):
        value = jnp.zeros((16, 128), F32)
        for n, x in enumerate(news):
            value = jnp.where(tile == n, x[z : z + 1], value)
        o_ref[z, 128:144, :] = value.astype(BF)


def fold(first, second):
    return pl.pallas_call(
        fold_kernel,
        out_shape=jax.ShapeDtypeStruct((8, 144, 128), BF),
        compiler_params=pltpu.CompilerParams(vmem_limit_bytes=24 * MIB),
        name="fold",
    )(first, second)


def prompt_kernel(where, slots, *refs):
    q_refs, kv_refs, o_ref, st_ref = refs[:8], refs[8:12], refs[12], refs[13]
    row, lane = eye_mask(64)
    query = where[1] * 4 + lax.broadcasted_iota(jnp.int32, (64, 64), 0) // 16
    column = lax.broadcasted_iota(jnp.int32, (64, 64), 1)
    mine = where[1] // 16
    for h in range(2):
        q = q_refs[4 * h][...]
        for j in range(1, 4):
            q = jnp.where(slots[j] == mine, q_refs[4 * h + j][...], q)
        scores = []
        for j in range(4):
            part = dot_nt(q, kv_refs[j][h * 128 : h * 128 + 64, :]) * SCALE
            seen = column + slots[j] * 64 <= query
            scores.append(jnp.where(seen, part, -jnp.inf))
        top = functools.reduce(jnp.maximum, [jnp.max(s, axis=1, keepdims=True) for s in scores])
        top = jnp.ceil(top)
        acc = jnp.zeros((64, 128), F32)
        total = jnp.zeros((64, 1), F32)
        for j in range(4):
            weights = jnp.exp2(scores[j] - top).astype(BF)
            total = total + jnp.sum(weights.astype(F32), axis=1, keepdims=True)
            acc = acc + dot_nn(weights, kv_refs[j][h * 128 + 64 : h * 128 + 128, :])
        o_ref[h] = acc.astype(BF)
        pair = jnp.where(lane == row, top, jnp.where(lane == row + 64, total, 0.0))
        st_ref[h] = jnp.broadcast_to(jnp.sum(pair, axis=0, keepdims=True), (8, 128))


def prompt_part(q_first, q_second, where, slots):
    q_spec = pl.BlockSpec((64, 128), lambda i, w, s: (w[0], 0))
    kv_spec = pl.BlockSpec((256, 128), lambda i, w, s: (4, 0))
    return pl.pallas_call(
        prompt_kernel,
        grid_spec=pltpu.PrefetchScalarGridSpec(
            num_scalar_prefetch=2,
            grid=(1,),
            in_specs=[q_spec] * 8 + [kv_spec] * 4,
            out_specs=[
                pl.BlockSpec((2, 64, 128), lambda i, w, s: (0, 0, 0)),
                pl.BlockSpec((2, 8, 128), lambda i, w, s: (0, 0, 0)),
            ],
        ),
        out_shape=[
            jax.ShapeDtypeStruct((2, 64, 128), BF),
            jax.ShapeDtypeStruct((2, 8, 128), F32),
        ],
        compiler_params=pltpu.CompilerParams(vmem_limit_bytes=16 * MIB),
        name="prompt",
    )(where, slots, *q_first, *q_second, *q_second)


def final_kernel(got_ref, po_ref, pst_ref, o_ref):
    row, lane = eye_mask(64)
    for h in range(2):
        stats = []
        for src in range(8):
            block = got_ref[src, 128:144, :].astype(F32)
            stats.append(block[2 * h : 2 * h + 1] + block[2 * h + 1 : 2 * h + 2])
        stats.append(pst_ref[h][0:1])
        peak, factors, sums = weigh(stats)
        total = functools.reduce(jnp.add, [f * s for f, s in zip(factors, sums)])
        inverse = 1.0 / jnp.where(lane[0:1] < 64, total, 1.0)
        factors = [f * inverse for f in factors]
        factors.append(jnp.zeros_like(inverse))
        mix = spread([pair_up(factors[2 * p], factors[2 * p + 1], lane) for p in range(5)], row, lane)
        parts = got_ref[:, h * 64 : h * 64 + 64, :].reshape(512, 128)
        parts = jnp.concatenate([parts, po_ref[h], jnp.zeros((64, 128), BF)], axis=0)
        high = mix.astype(BF)
        low = (mix - high.astype(F32)).astype(BF)
        out = dot_nn(high, parts) + dot_nn(low, parts)
        o_ref[:, h * 16 : h * 16 + 16, :] = out.astype(BF).reshape(4, 16, 128)


def final(got, part_out, part_stats):
    return pl.pallas_call(
        final_kernel,
        out_shape=jax.ShapeDtypeStruct((4, 32, 128), BF),
        compiler_params=pltpu.CompilerParams(vmem_limit_bytes=16 * MIB),
        name="final",
    )(got, part_out, part_stats)


def body(
    queries,
    prompt_keys,
    prompt_values,
    cache_keys,
    cache_values,
    cache_lengths,
    offset,
    prompt_positions,
):
    axes = ("context", "tensor")
    context = lax.axis_index("context").astype(jnp.int32)
    tensor = lax.axis_index("tensor").astype(jnp.int32)
    core = tensor % 2
    other = 2 * (1 - tensor // 2)
    sends = jnp.stack([tensor, tensor ^ 1, other + core, other + 1 - core])
    slots = sends

    position = offset[0] + prompt_positions
    freq = jnp.exp(jnp.arange(64, dtype=F32) * (-2.0 * math.log(500000.0) / 128))
    angle = position.astype(F32)[:, None] * freq[None, :]
    cosine = jnp.cos(angle)
    sine = jnp.sin(angle)
    cosine = jnp.concatenate([cosine, cosine], axis=1)
    sine = jnp.concatenate([-sine, sine], axis=1)
    wide = prompt_keys.astype(F32)
    turned = wide * cosine[:, None, :] + jnp.roll(wide, 64, axis=-1) * sine[:, None, :]
    kv = jnp.stack([turned.astype(BF), prompt_values]).transpose(2, 0, 1, 3)

    def exchange(parts):
        own, swap, ahead, back = parts
        return (
            own,
            lax.ppermute(swap, axes, shift(0, 1)),
            lax.ppermute(ahead, axes, shift(1, 0)),
            lax.ppermute(back, axes, shift(-1, 1)),
        )

    q_first = exchange(turn(queries, cosine, sine, None, sends, 0))
    q_second = exchange(turn(queries, cosine, sine, kv, sends, 1))

    keys = cache_keys.transpose(1, 0, 2)
    values = cache_values.transpose(1, 0, 2)

    plane = [[z * 8 + r for r in range(8)] for z in range(8)]
    column = [[z * 8 + r for z in range(8)] for r in range(8)]

    def swap(parts, groups):
        return lax.all_to_all(
            parts, "context", split_axis=0, concat_axis=0, axis_index_groups=groups, tiled=True
        )

    first = swap(attend(q_first, keys, values, slots, cache_lengths, 0), plane)
    second = swap(attend(q_second, keys, values, slots, cache_lengths, 1), plane)
    where = jnp.stack([context % 16, context])
    part_out, part_stats = prompt_part(q_first, q_second, where, slots)
    got = swap(fold(first, second), column)
    return final(got, part_out, part_stats)


def solution(mesh):
    in_specs = (
        P("tensor", None, None),
        P("tensor", None, None),
        P("tensor", None, None),
        P("context", "tensor", None),
        P("context", "tensor", None),
        P("context"),
        P(),
        P("tensor"),
    )
    out_specs = P("context", "tensor", None)
    return jax.shard_map(body, mesh=mesh, in_specs=in_specs, out_specs=out_specs, check_vma=False)
```

```python
import functools
import math

import jax
import jax.numpy as jnp
import numpy as np
from jax import lax
from jax.experimental import pallas as pl
from jax.experimental.pallas import tpu as pltpu
from jax.sharding import PartitionSpec as P

SCALE = math.log2(math.e) / math.sqrt(128.0)
BF = jnp.bfloat16
F32 = jnp.float32
MIB = 2**20
BIG = 60 * MIB
KEY_BLOCK = 512
SUB = 256


def linear(z, x, y, core):
    y = y % 4
    return ((z % 8) * 8 + (x % 4) * 2 + y // 2) * 4 + (y % 2) * 2 + core % 2


def shift(dy, dcore):
    return [
        (linear(z, x, y, k), linear(z, x, y + dy, k + dcore))
        for z in range(8)
        for x in range(4)
        for y in range(4)
        for k in range(2)
    ]


def dot_nt(a, b):
    return lax.dot_general(a, b, (((1,), (1,)), ((), ())), preferred_element_type=F32)


def dot_nn(a, b):
    return jnp.dot(a, b, preferred_element_type=F32)


def slots_of():
    tensor = lax.axis_index("tensor").astype(jnp.int32)
    core = lax.rem(tensor, 2)
    other = 2 * (1 - lax.div(tensor, 2))
    return tensor, tensor + 1 - 2 * core, other + core, other + 1 - core


def turn_kernel(offset, pos_ref, freq_ref, k_ref, v_ref, q_ref, *refs):
    outs, (q_s, out_s, cos_s, sin_s, wide_s, in_sem, out_sem) = refs[:4], refs[4:]
    slots = slots_of()

    def fetch(j):
        heads = pl.ds(pl.multiple_of(slots[j] * 32, 32), 32)
        return pltpu.make_async_copy(q_ref.at[:, heads, :], q_s.at[j], in_sem.at[j])

    def send(j):
        return pltpu.make_async_copy(out_s.at[j], outs[j], out_sem.at[j])

    order = (2, 3, 1, 0)
    for j in order:
        fetch(j).start()
    row = lax.broadcasted_iota(jnp.int32, (64, 64), 0)
    column = lax.broadcasted_iota(jnp.int32, (64, 64), 1)
    position = (pos_ref[...] + offset[0]).astype(F32)
    position = jnp.sum(jnp.where(row == column, position, 0.0), axis=1, keepdims=True)
    angle = position * freq_ref[...]
    lane = lax.broadcasted_iota(jnp.int32, (64, 128), 1)
    cosine = jnp.cos(angle)
    sine = jnp.sin(angle)
    sine = jnp.where(lane < 64, -sine, sine)
    cos_s[...] = cosine
    sin_s[...] = sine
    wide = k_ref[...].astype(F32)
    rolled = pltpu.roll(wide.reshape(512, 128), 64, 1).reshape(64, 8, 128)
    wide_s[0] = (wide * cosine[:, None, :] + rolled * sine[:, None, :]).reshape(512, 128)
    wide_s[1] = v_ref[...].astype(F32).reshape(512, 128)
    for j in order:
        fetch(j).wait()

        @pl.loop(0, 4)
        def _(i):
            rows = pl.ds(pl.multiple_of(i * 16, 16), 16)
            cosine = cos_s[rows, :][:, None, :]
            sine = sin_s[rows, :][:, None, :]
            for head in range(2):
                wide = q_s[j, rows, head * 16 : head * 16 + 16, :].astype(F32)
                rolled = pltpu.roll(wide.reshape(256, 128), 64, 1).reshape(16, 16, 128)
                value = (wide * cosine + rolled * sine).reshape(256, 128).astype(BF)
                out_s[j, pl.ds(pl.multiple_of(head * 1024 + i * 256, 256), 256), :] = value

        for head in range(2):
            for n in range(2):
                start = 2048 + head * 128 + n * 64
                picked = wide_s[n, pl.ds(2 * slots[j] + head, 64, 8), :]
                out_s[j, start : start + 64, :] = picked.astype(BF)
        send(j).start()
    for j in order:
        send(j).wait()


def turn(queries, offset, positions, keys, values):
    freq = np.exp(np.arange(64, dtype=np.float32) * np.float32(-2.0 * math.log(500000.0) / 128))
    freq = jnp.asarray(np.concatenate([freq, freq])[None, :], F32)
    vmem = pl.BlockSpec(memory_space=pltpu.VMEM)
    hbm = pl.BlockSpec(memory_space=pl.ANY)
    return pl.pallas_call(
        turn_kernel,
        in_specs=[pl.BlockSpec(memory_space=pltpu.SMEM)] + [vmem] * 4 + [hbm],
        out_specs=[hbm] * 4,
        out_shape=[jax.ShapeDtypeStruct((2304, 128), BF)] * 4,
        scratch_shapes=[
            pltpu.VMEM((4, 64, 32, 128), BF),
            pltpu.VMEM((4, 2304, 128), BF),
            pltpu.VMEM((64, 128), F32),
            pltpu.VMEM((64, 128), F32),
            pltpu.VMEM((2, 512, 128), F32),
            pltpu.SemaphoreType.DMA((4,)),
            pltpu.SemaphoreType.DMA((4,)),
        ],
        compiler_params=pltpu.CompilerParams(vmem_limit_bytes=BIG),
        name="turn",
    )(offset, positions.reshape(1, 64), freq, keys, values, queries)


def lay_kernel(length, k_ref, v_ref, ko_ref, vo_ref, in_s, wide_s, out_s, in_sem, out_sem):
    refs, outs = (k_ref, v_ref), (ko_ref, vo_ref)

    def fetch(n, c):
        rows = pl.ds(c * 1024, 1024)
        return pltpu.make_async_copy(refs[n].at[rows, :], in_s.at[n, rows, :], in_sem.at[n, c])

    def send(n, c):
        rows = pl.ds(c * 512, 512)
        return pltpu.make_async_copy(
            out_s.at[n, :, rows, :], outs[n].at[:, rows, :], out_sem.at[n, c]
        )

    parts = [(n, c) for c in range(4) for n in range(2)]
    for n, c in parts:
        fetch(n, c).start()
    for n, c in parts:
        fetch(n, c).wait()
        live = lax.broadcasted_iota(jnp.int32, (512, 128), 0) + c * 512 < length[0]
        wide_s[n] = in_s[n, c * 1024 : c * 1024 + 1024, :].astype(F32)
        first = in_s[n, 0:16, :].astype(F32)
        for head in range(2):
            value = wide_s[n, pl.ds(head, 512, 2), :]
            dead = first[head : head + 1, :] if n == 0 else 0.0
            out_s[n, head, c * 512 : c * 512 + 512, :] = jnp.where(live, value, dead).astype(BF)
        send(n, c).start()
    for n, c in parts:
        send(n, c).wait()


def lay(keys, values, length):
    return pl.pallas_call(
        lay_kernel,
        in_specs=[pl.BlockSpec(memory_space=pltpu.SMEM)] + [pl.BlockSpec(memory_space=pl.ANY)] * 2,
        out_specs=[pl.BlockSpec(memory_space=pl.ANY)] * 2,
        out_shape=[jax.ShapeDtypeStruct((2, 2048, 128), BF)] * 2,
        scratch_shapes=[
            pltpu.VMEM((2, 4096, 128), BF),
            pltpu.VMEM((2, 1024, 128), F32),
            pltpu.VMEM((2, 2, 2048, 128), BF),
            pltpu.SemaphoreType.DMA((2, 4)),
            pltpu.SemaphoreType.DMA((2, 4)),
        ],
        compiler_params=pltpu.CompilerParams(vmem_limit_bytes=24 * MIB),
        name="lay",
    )(length, keys.reshape(4096, 128), values.reshape(4096, 128))


def eye_mask(rows):
    row = lax.broadcasted_iota(jnp.int32, (rows, 128), 0)
    lane = lax.broadcasted_iota(jnp.int32, (rows, 128), 1)
    return row, lane


def attend_kernel(length, q0, q1, k_ref, v_ref, *refs, base):
    o_ref, q_s, k_s, v_s, o_s, st_s, q_sem, kv_sem, o_sem, st_sem = refs[-10:]
    core = lax.rem(lax.axis_index("tensor").astype(jnp.int32), 2)

    def fetch_q(j):
        return pltpu.make_async_copy((q0, q1)[j].at[pl.ds(0, 2048), :], q_s.at[j], q_sem.at[j])

    def fetch_kv(head, c):
        rows = pl.ds(c * 1024, 1024)
        return (
            pltpu.make_async_copy(
                k_ref.at[head, rows, :], k_s.at[head, rows, :], kv_sem.at[head, 0, c]
            ),
            pltpu.make_async_copy(
                v_ref.at[head, rows, :], v_s.at[head, rows, pl.ds(0, 128)], kv_sem.at[head, 1, c]
            ),
        )

    def place(j):
        return 2 * (core + j * (1 - 2 * core))

    def send(head, j, half):
        start = pl.multiple_of((2 * (place(j) + half) + head) * 64, 64)
        return pltpu.make_async_copy(
            o_s.at[:, pl.ds(start, 64), :],
            o_ref.at[:, pl.ds(pl.multiple_of(base + start, 16), 64), :],
            o_sem.at[2 * head + j, half],
        )

    for copy in fetch_kv(0, 0) + fetch_kv(0, 1) + (fetch_q(0), fetch_q(1)):
        copy.start()
    for copy in fetch_kv(1, 0) + fetch_kv(1, 1):
        copy.start()
    live = lax.broadcasted_iota(jnp.int32, (2048, 128), 0) < length[0]
    live = jnp.where(live, 1.0, 0.0).astype(BF)
    v_s[0, :, 128:256] = live
    v_s[1, :, 128:256] = live
    for copy in fetch_kv(0, 0) + fetch_kv(0, 1) + (fetch_q(0), fetch_q(1)):
        copy.wait()
    row, lane = eye_mask(64)

    @pl.loop(0, 4)
    def _(step):
        head = step // 2
        j = step % 2

        @pl.when(step == 2)
        def _():
            for copy in fetch_kv(1, 0) + fetch_kv(1, 1):
                copy.wait()

        for s in range(4):
            q = q_s[j, pl.ds(pl.multiple_of(head * 1024 + s * SUB, SUB), SUB), :]
            peak = None
            for b in range(2048 // KEY_BLOCK):
                keys = slice(b * KEY_BLOCK, (b + 1) * KEY_BLOCK)
                scores = dot_nt(q, k_s[head, keys, :])
                top = jnp.ceil(jnp.max(scores, axis=1, keepdims=True) * SCALE)
                new = top if peak is None else jnp.maximum(peak, top)
                weights = jnp.exp2(scores * SCALE - new).astype(BF)
                part = dot_nn(weights, v_s[head, keys, :])
                acc = part if peak is None else acc * jnp.exp2(peak - new) + part
                peak = new
            unit = 2 * (place(j) + s // 2) + head
            for d in range(4):
                dest = 4 * (s % 2) + d
                rows = slice(d * 64, (d + 1) * 64)
                to = pl.ds(pl.multiple_of(unit * 64, 64), 64)
                o_s[dest, to, :] = acc[rows, 0:128].astype(BF)
                pair = jnp.where(
                    lane == row,
                    peak[rows, :],
                    jnp.where(lane == row + 64, acc[rows, 128:256], 0.0),
                )
                st_s[dest, pl.ds(unit, 1), :] = jnp.sum(pair, axis=0, keepdims=True)
        send(head, j, 0).start()
        send(head, j, 1).start()

    for dest in range(8):
        stats = st_s[dest]
        high = stats.astype(BF).astype(F32)
        o_s[dest, 512:528, :] = jnp.concatenate([high, stats - high], axis=0).astype(BF)
    tail = pltpu.make_async_copy(
        o_s.at[:, pl.ds(512, 16), :], o_ref.at[:, pl.ds(base + 512, 16), :], st_sem
    )
    tail.start()
    for head in range(2):
        for j in range(2):
            for half in range(2):
                send(head, j, half).wait()
    tail.wait()


def attend(qs, keys, values, length, before, name):
    any_space = pl.BlockSpec(memory_space=pl.ANY)
    args = [length, *qs, keys, values]
    aliases = {}
    if before is not None:
        aliases = {len(args): 0}
        args.append(before)
    return pl.pallas_call(
        functools.partial(attend_kernel, base=0 if before is None else 528),
        in_specs=[pl.BlockSpec(memory_space=pltpu.SMEM)] + [any_space] * (len(args) - 1),
        out_specs=any_space,
        scratch_shapes=[
            pltpu.VMEM((2, 2048, 128), BF),
            pltpu.VMEM((2, 2048, 128), BF),
            pltpu.VMEM((2, 2048, 256), BF),
            pltpu.VMEM((8, 528, 128), BF),
            pltpu.VMEM((8, 8, 128), F32),
            pltpu.SemaphoreType.DMA((2,)),
            pltpu.SemaphoreType.DMA((2, 2, 2)),
            pltpu.SemaphoreType.DMA((4, 2)),
            pltpu.SemaphoreType.DMA(()),
        ],
        out_shape=jax.ShapeDtypeStruct((8, 1056, 128), BF),
        input_output_aliases=aliases,
        compiler_params=pltpu.CompilerParams(vmem_limit_bytes=40 * MIB),
        cost_estimate=pl.CostEstimate(
            flops=4 * 4096 * 2048 * 128, bytes_accessed=4 * MIB, transcendentals=4096 * 2048
        ),
        name=name,
    )(*args)


def weigh(stats):
    peak = functools.reduce(jnp.maximum, stats)
    factors = [jnp.exp2(s - peak) for s in stats]
    sums = [pltpu.roll(s, 64, 1) for s in stats]
    return peak, factors, sums


def spread(pairs, row, lane):
    hit = (lane == row) | (lane == row + 64)
    return jnp.concatenate([jnp.where(hit, p, 0.0) for p in pairs], axis=1)


def pair_up(first, second, lane):
    return jnp.where(lane[0:1] < 64, first, pltpu.roll(second, 64, 1))


def fold_kernel(in_ref, out_ref, o_ref, sem):
    half = lax.div(lax.axis_index("tensor").astype(jnp.int32), 2)
    halves = (half, 1 - half)
    row, lane = eye_mask(64)
    lane8 = lax.broadcasted_iota(jnp.int32, (8, 128), 1)
    tile = lax.broadcasted_iota(jnp.int32, (16, 128), 0)
    for n in range(2):
        base = 528 * n
        stats = []
        for src in range(8):
            block = in_ref[src, base + 512 : base + 528, :].astype(F32)
            stats.append(block[0:8] + block[8:16])
        peak, factors, sums = weigh(stats)
        factors = [f.astype(BF).astype(F32) for f in factors]
        total = functools.reduce(jnp.add, [f * s for f, s in zip(factors, sums)])
        rolled = [pltpu.roll(f, 64, 1) for f in factors]
        joined = [jnp.where(lane8 < 64, factors[2 * p], rolled[2 * p + 1]) for p in range(4)]
        new = jnp.where(lane8 < 64, peak, pltpu.roll(total, 64, 1))
        high = new.astype(BF).astype(F32)
        low = new - high
        for zl in range(4):
            z = halves[n] * 4 + zl
            value = jnp.zeros((16, 128), F32)
            for head in range(2):
                unit = 2 * zl + head
                mix = spread([x[unit : unit + 1] for x in joined], row, lane).astype(BF)
                at = base + unit * 64
                parts = in_ref[:, at : at + 64, :].reshape(512, 128)
                o_ref[z, head * 64 : head * 64 + 64, :] = dot_nn(mix, parts).astype(BF)
                value = jnp.where(tile == 2 * head, high[unit : unit + 1], value)
                value = jnp.where(tile == 2 * head + 1, low[unit : unit + 1], value)
            o_ref[z, 128:144, :] = value.astype(BF)
            pltpu.make_async_copy(o_ref.at[z], out_ref.at[z], sem.at[4 * n + zl]).start()
    for n in range(2):
        for zl in range(4):
            z = halves[n] * 4 + zl
            pltpu.make_async_copy(o_ref.at[z], out_ref.at[z], sem.at[4 * n + zl]).wait()


def fold(parts):
    return pl.pallas_call(
        fold_kernel,
        in_specs=[pl.BlockSpec(memory_space=pltpu.VMEM)],
        out_specs=pl.BlockSpec(memory_space=pl.ANY),
        out_shape=jax.ShapeDtypeStruct((8, 144, 128), BF),
        scratch_shapes=[pltpu.VMEM((8, 144, 128), BF), pltpu.SemaphoreType.DMA((8,))],
        compiler_params=pltpu.CompilerParams(vmem_limit_bytes=24 * MIB),
        name="fold",
    )(parts)


def prompt_kernel(where, slots, *refs):
    q_refs, kv_refs, o_ref, st_ref = refs[:8], refs[8:12], refs[12], refs[13]
    row, lane = eye_mask(64)
    query = where[1] * 4 + lax.broadcasted_iota(jnp.int32, (64, 64), 0) // 16
    column = lax.broadcasted_iota(jnp.int32, (64, 64), 1)
    mine = where[1] // 16
    for h in range(2):
        q = q_refs[4 * h][...]
        for j in range(1, 4):
            q = jnp.where(slots[j] == mine, q_refs[4 * h + j][...], q)
        scores = []
        for j in range(4):
            part = dot_nt(q, kv_refs[j][h * 128 : h * 128 + 64, :]) * SCALE
            seen = column + slots[j] * 64 <= query
            scores.append(jnp.where(seen, part, -jnp.inf))
        top = functools.reduce(jnp.maximum, [jnp.max(s, axis=1, keepdims=True) for s in scores])
        top = jnp.ceil(top)
        acc = jnp.zeros((64, 128), F32)
        total = jnp.zeros((64, 1), F32)
        for j in range(4):
            weights = jnp.exp2(scores[j] - top).astype(BF)
            total = total + jnp.sum(weights.astype(F32), axis=1, keepdims=True)
            acc = acc + dot_nn(weights, kv_refs[j][h * 128 + 64 : h * 128 + 128, :])
        o_ref[h] = acc.astype(BF)
        pair = jnp.where(lane == row, top, jnp.where(lane == row + 64, total, 0.0))
        st_ref[h] = jnp.broadcast_to(jnp.sum(pair, axis=0, keepdims=True), (8, 128))


def prompt_part(qs, where, slots):
    first = pl.BlockSpec((64, 128), lambda i, w, s: (w[0], 0))
    second = pl.BlockSpec((64, 128), lambda i, w, s: (16 + w[0], 0))
    kv_spec = pl.BlockSpec((256, 128), lambda i, w, s: (8, 0))
    return pl.pallas_call(
        prompt_kernel,
        grid_spec=pltpu.PrefetchScalarGridSpec(
            num_scalar_prefetch=2,
            grid=(1,),
            in_specs=[first] * 4 + [second] * 4 + [kv_spec] * 4,
            out_specs=[
                pl.BlockSpec((2, 64, 128), lambda i, w, s: (0, 0, 0)),
                pl.BlockSpec((2, 8, 128), lambda i, w, s: (0, 0, 0)),
            ],
        ),
        out_shape=[
            jax.ShapeDtypeStruct((2, 64, 128), BF),
            jax.ShapeDtypeStruct((2, 8, 128), F32),
        ],
        compiler_params=pltpu.CompilerParams(vmem_limit_bytes=40 * MIB),
        name="prompt",
    )(where, slots, *qs, *qs, *qs)


def final_kernel(got_ref, po_ref, pst_ref, o_ref):
    row, lane = eye_mask(64)
    for h in range(2):
        stats = []
        for src in range(8):
            block = got_ref[src, 128:144, :].astype(F32)
            stats.append(block[2 * h : 2 * h + 1] + block[2 * h + 1 : 2 * h + 2])
        stats.append(pst_ref[h][0:1])
        peak, factors, sums = weigh(stats)
        total = functools.reduce(jnp.add, [f * s for f, s in zip(factors, sums)])
        inverse = 1.0 / jnp.where(lane[0:1] < 64, total, 1.0)
        factors = [f * inverse for f in factors]
        factors.append(jnp.zeros_like(inverse))
        mix = spread([pair_up(factors[2 * p], factors[2 * p + 1], lane) for p in range(5)], row, lane)
        parts = got_ref[:, h * 64 : h * 64 + 64, :].reshape(512, 128)
        parts = jnp.concatenate([parts, po_ref[h], jnp.zeros((64, 128), BF)], axis=0)
        high = mix.astype(BF)
        low = (mix - high.astype(F32)).astype(BF)
        out = dot_nn(high, parts) + dot_nn(low, parts)
        o_ref[:, h * 16 : h * 16 + 16, :] = out.astype(BF).reshape(4, 16, 128)


def final(got, part_out, part_stats):
    return pl.pallas_call(
        final_kernel,
        out_shape=jax.ShapeDtypeStruct((4, 32, 128), BF),
        compiler_params=pltpu.CompilerParams(vmem_limit_bytes=16 * MIB),
        name="final",
    )(got, part_out, part_stats)


def body(
    queries,
    prompt_keys,
    prompt_values,
    cache_keys,
    cache_values,
    cache_lengths,
    offset,
    prompt_positions,
):
    axes = ("context", "tensor")
    context = lax.axis_index("context").astype(jnp.int32)
    own, swapped, ahead, back = turn(queries, offset, prompt_positions, prompt_keys, prompt_values)
    ahead = lax.ppermute(ahead, axes, shift(1, 0))
    back = lax.ppermute(back, axes, shift(-1, 1))
    swapped = lax.ppermute(swapped, axes, shift(0, 1))
    keys, values = lay(cache_keys, cache_values, cache_lengths)

    plane = [[z * 8 + r for r in range(8)] for z in range(8)]
    column = [[z * 8 + r for z in range(8)] for r in range(8)]

    def swap(parts, groups):
        return lax.all_to_all(
            parts, "context", split_axis=0, concat_axis=0, axis_index_groups=groups, tiled=True
        )

    parts = attend((own, swapped), keys, values, cache_lengths, None, "near")
    parts = attend((ahead, back), keys, values, cache_lengths, parts, "far")
    parts = swap(parts, plane)
    where = jnp.stack([context % 16, context])
    slots = jnp.stack(slots_of())
    part_out, part_stats = prompt_part((own, swapped, ahead, back), where, slots)
    got = swap(fold(parts), column)
    return final(got, part_out, part_stats)


def solution(mesh):
    in_specs = (
        P("tensor", None, None),
        P("tensor", None, None),
        P("tensor", None, None),
        P("context", "tensor", None),
        P("context", "tensor", None),
        P("context"),
        P(),
        P("tensor"),
    )
    out_specs = P("context", "tensor", None)
    return jax.shard_map(body, mesh=mesh, in_specs=in_specs, out_specs=out_specs, check_vma=False)
```

```python
import functools
import math

import jax
import jax.numpy as jnp
import numpy as np
from jax import lax
from jax.experimental import pallas as pl
from jax.experimental.pallas import tpu as pltpu
from jax.sharding import PartitionSpec as P

SCALE = math.log2(math.e) / math.sqrt(128.0)
BF = jnp.bfloat16
F32 = jnp.float32
MIB = 2**20
BIG = 60 * MIB
KEY_BLOCK = 512
SUB = 256


def linear(z, x, y, core):
    y = y % 4
    return ((z % 8) * 8 + (x % 4) * 2 + y // 2) * 4 + (y % 2) * 2 + core % 2


def shift(dy, dcore):
    return [
        (linear(z, x, y, k), linear(z, x, y + dy, k + dcore))
        for z in range(8)
        for x in range(4)
        for y in range(4)
        for k in range(2)
    ]


def dot_nt(a, b):
    return lax.dot_general(a, b, (((1,), (1,)), ((), ())), preferred_element_type=F32)


def dot_nn(a, b):
    return jnp.dot(a, b, preferred_element_type=F32)


def slots_of():
    tensor = lax.axis_index("tensor").astype(jnp.int32)
    core = lax.rem(tensor, 2)
    other = 2 * (1 - lax.div(tensor, 2))
    return tensor, tensor + 1 - 2 * core, other + core, other + 1 - core


def turn_kernel(offset, pos_ref, freq_ref, k_ref, v_ref, q_ref, *refs):
    outs, (q_s, out_s, cos_s, sin_s, wide_s, in_sem, out_sem) = refs[:4], refs[4:]
    slots = slots_of()

    def fetch(j):
        heads = pl.ds(pl.multiple_of(slots[j] * 32, 32), 32)
        return pltpu.make_async_copy(q_ref.at[:, heads, :], q_s.at[j], in_sem.at[j])

    def send(j):
        return pltpu.make_async_copy(out_s.at[j], outs[j], out_sem.at[j])

    order = (2, 3, 1, 0)
    for j in order:
        fetch(j).start()
    row = lax.broadcasted_iota(jnp.int32, (64, 64), 0)
    column = lax.broadcasted_iota(jnp.int32, (64, 64), 1)
    position = (pos_ref[...] + offset[0]).astype(F32)
    position = jnp.sum(jnp.where(row == column, position, 0.0), axis=1, keepdims=True)
    left = lax.broadcasted_iota(jnp.int32, (32, 128), 1) < 64
    angle = jnp.where(left, position[0:32], position[32:64]) * freq_ref[...]
    both = []
    for value in (jnp.cos(angle), jnp.sin(angle)):
        moved = pltpu.roll(value, 64, 1)
        above = jnp.where(left, value, moved)
        below = jnp.where(left, moved, value)
        both.append(jnp.concatenate([above, below], axis=0))
    lane = lax.broadcasted_iota(jnp.int32, (64, 128), 1)
    cosine = both[0]
    sine = jnp.where(lane < 64, -both[1], both[1])
    cos_s[...] = cosine
    sin_s[...] = sine
    wide = k_ref[...].astype(F32)
    rolled = pltpu.roll(wide.reshape(512, 128), 64, 1).reshape(64, 8, 128)
    wide_s[0] = (wide * cosine[:, None, :] + rolled * sine[:, None, :]).reshape(512, 128)
    wide_s[1] = v_ref[...].astype(F32).reshape(512, 128)
    for j in order:
        fetch(j).wait()

        @pl.loop(0, 4, unroll=True)
        def _(i):
            rows = pl.ds(pl.multiple_of(i * 16, 16), 16)
            cosine = cos_s[rows, :][:, None, :]
            sine = sin_s[rows, :][:, None, :]
            for head in range(2):
                wide = q_s[j, rows, head * 16 : head * 16 + 16, :].astype(F32)
                rolled = pltpu.roll(wide.reshape(256, 128), 64, 1).reshape(16, 16, 128)
                value = (wide * cosine + rolled * sine).reshape(256, 128).astype(BF)
                out_s[j, pl.ds(pl.multiple_of(head * 1024 + i * 256, 256), 256), :] = value

        for head in range(2):
            for n in range(2):
                start = 2048 + head * 128 + n * 64
                picked = wide_s[n, pl.ds(2 * slots[j] + head, 64, 8), :]
                out_s[j, start : start + 64, :] = picked.astype(BF)
        send(j).start()
    for j in order:
        send(j).wait()


def turn(queries, offset, positions, keys, values):
    freq = np.exp(np.arange(64, dtype=np.float32) * np.float32(-2.0 * math.log(500000.0) / 128))
    freq = jnp.asarray(np.concatenate([freq, freq])[None, :], F32)
    vmem = pl.BlockSpec(memory_space=pltpu.VMEM)
    hbm = pl.BlockSpec(memory_space=pl.ANY)
    return pl.pallas_call(
        turn_kernel,
        in_specs=[pl.BlockSpec(memory_space=pltpu.SMEM)] + [vmem] * 4 + [hbm],
        out_specs=[hbm] * 4,
        out_shape=[jax.ShapeDtypeStruct((2304, 128), BF)] * 4,
        scratch_shapes=[
            pltpu.VMEM((4, 64, 32, 128), BF),
            pltpu.VMEM((4, 2304, 128), BF),
            pltpu.VMEM((64, 128), F32),
            pltpu.VMEM((64, 128), F32),
            pltpu.VMEM((2, 512, 128), F32),
            pltpu.SemaphoreType.DMA((4,)),
            pltpu.SemaphoreType.DMA((4,)),
        ],
        compiler_params=pltpu.CompilerParams(vmem_limit_bytes=BIG),
        name="turn",
    )(offset, positions.reshape(1, 64), freq, keys, values, queries)


def lay_kernel(length, k_ref, v_ref, ko_ref, vo_ref, wide_s):
    for c in range(4):
        live = lax.broadcasted_iota(jnp.int32, (512, 128), 0) + c * 512 < length[0]
        rows = slice(c * 512, c * 512 + 512)
        wide_s[0] = k_ref[c * 1024 : c * 1024 + 1024, :].astype(F32)
        wide_s[1] = v_ref[c * 1024 : c * 1024 + 1024, :].astype(F32)
        first = k_ref[0:16, :].astype(F32)
        one = jnp.where(live, 1.0, 0.0).astype(BF)
        for head in range(2):
            keys = wide_s[0, pl.ds(head, 512, 2), :]
            values = wide_s[1, pl.ds(head, 512, 2), :]
            ko_ref[head, rows, :] = jnp.where(live, keys, first[head : head + 1, :]).astype(BF)
            vo_ref[head, rows, 0:128] = jnp.where(live, values, 0.0).astype(BF)
            vo_ref[head, rows, 128:256] = one


def lay(keys, values, length):
    vmem = pl.BlockSpec(memory_space=pltpu.VMEM)
    return pl.pallas_call(
        lay_kernel,
        in_specs=[pl.BlockSpec(memory_space=pltpu.SMEM), vmem, vmem],
        out_specs=[vmem, vmem],
        out_shape=[
            jax.ShapeDtypeStruct((2, 2048, 128), BF),
            jax.ShapeDtypeStruct((2, 2048, 256), BF),
        ],
        scratch_shapes=[pltpu.VMEM((2, 1024, 128), F32)],
        compiler_params=pltpu.CompilerParams(vmem_limit_bytes=24 * MIB),
        name="lay",
    )(length, keys.reshape(4096, 128), values.reshape(4096, 128))


def eye_mask(rows):
    row = lax.broadcasted_iota(jnp.int32, (rows, 128), 0)
    lane = lax.broadcasted_iota(jnp.int32, (rows, 128), 1)
    return row, lane


def attend_kernel(q0, q1, k_ref, v_ref, *refs, base):
    o_ref, q_s, o_s, st_s, o_sem, st_sem = refs[-6:]
    core = lax.rem(lax.axis_index("tensor").astype(jnp.int32), 2)

    def place(j):
        return 2 * (core + j * (1 - 2 * core))

    def send(head, j, half):
        start = pl.multiple_of((2 * (place(j) + half) + head) * 64, 64)
        return pltpu.make_async_copy(
            o_s.at[:, pl.ds(start, 64), :],
            o_ref.at[:, pl.ds(pl.multiple_of(base + start, 16), 64), :],
            o_sem.at[2 * head + j, half],
        )

    row, lane = eye_mask(64)

    @pl.loop(0, 4)
    def _(step):
        head = step // 2
        j = step % 2

        for n, ref in enumerate((q0, q1)):

            @pl.when(j == n)
            def _():
                q_s[...] = ref[pl.ds(pl.multiple_of(head * 1024, 1024), 1024), :]

        for s in range(4):
            q = q_s[s * SUB : (s + 1) * SUB, :]
            peak = None
            for b in range(2048 // KEY_BLOCK):
                keys = slice(b * KEY_BLOCK, (b + 1) * KEY_BLOCK)
                scores = dot_nt(q, k_ref[head, keys, :])
                top = jnp.ceil(jnp.max(scores, axis=1, keepdims=True) * SCALE)
                new = top if peak is None else jnp.maximum(peak, top)
                weights = jnp.exp2(scores * SCALE - new).astype(BF)
                part = dot_nn(weights, v_ref[head, keys, :])
                acc = part if peak is None else acc * jnp.exp2(peak - new) + part
                peak = new
            unit = 2 * (place(j) + s // 2) + head
            for d in range(4):
                dest = 4 * (s % 2) + d
                rows = slice(d * 64, (d + 1) * 64)
                to = pl.ds(pl.multiple_of(unit * 64, 64), 64)
                o_s[dest, to, :] = acc[rows, 0:128].astype(BF)
                pair = jnp.where(
                    lane == row,
                    peak[rows, :],
                    jnp.where(lane == row + 64, acc[rows, 128:256], 0.0),
                )
                st_s[dest, pl.ds(unit, 1), :] = jnp.sum(pair, axis=0, keepdims=True)
        send(head, j, 0).start()
        send(head, j, 1).start()

    for dest in range(8):
        stats = st_s[dest]
        high = stats.astype(BF).astype(F32)
        o_s[dest, 512:528, :] = jnp.concatenate([high, stats - high], axis=0).astype(BF)
    tail = pltpu.make_async_copy(
        o_s.at[:, pl.ds(512, 16), :], o_ref.at[:, pl.ds(base + 512, 16), :], st_sem
    )
    tail.start()
    for head in range(2):
        for j in range(2):
            for half in range(2):
                send(head, j, half).wait()
    tail.wait()


def attend(qs, keys, values, before, name):
    any_space = pl.BlockSpec(memory_space=pl.ANY)
    args = [*qs, keys, values]
    aliases = {}
    if before is not None:
        aliases = {len(args): 0}
        args.append(before)
    return pl.pallas_call(
        functools.partial(attend_kernel, base=0 if before is None else 528),
        in_specs=[pl.BlockSpec(memory_space=pltpu.VMEM)] * 4 + [any_space] * (len(args) - 4),
        out_specs=any_space,
        scratch_shapes=[
            pltpu.VMEM((1024, 128), BF),
            pltpu.VMEM((8, 528, 128), BF),
            pltpu.VMEM((8, 8, 128), F32),
            pltpu.SemaphoreType.DMA((4, 2)),
            pltpu.SemaphoreType.DMA(()),
        ],
        out_shape=jax.ShapeDtypeStruct((8, 1056, 128), BF),
        input_output_aliases=aliases,
        compiler_params=pltpu.CompilerParams(vmem_limit_bytes=40 * MIB),
        cost_estimate=pl.CostEstimate(
            flops=4 * 4096 * 2048 * 128, bytes_accessed=4 * MIB, transcendentals=4096 * 2048
        ),
        name=name,
    )(*args)


def weigh(stats):
    peak = functools.reduce(jnp.maximum, stats)
    factors = [jnp.exp2(s - peak) for s in stats]
    sums = [pltpu.roll(s, 64, 1) for s in stats]
    return peak, factors, sums


def spread(pairs, row, lane):
    hit = (lane == row) | (lane == row + 64)
    return jnp.concatenate([jnp.where(hit, p, 0.0) for p in pairs], axis=1)


def pair_up(first, second, lane):
    return jnp.where(lane[0:1] < 64, first, pltpu.roll(second, 64, 1))


def fold_kernel(in_ref, out_ref, o_ref, sem):
    half = lax.div(lax.axis_index("tensor").astype(jnp.int32), 2)
    halves = (half, 1 - half)
    row, lane = eye_mask(64)
    lane8 = lax.broadcasted_iota(jnp.int32, (8, 128), 1)
    tile = lax.broadcasted_iota(jnp.int32, (16, 128), 0)
    for n in range(2):
        base = 528 * n
        stats = []
        for src in range(8):
            block = in_ref[src, base + 512 : base + 528, :].astype(F32)
            stats.append(block[0:8] + block[8:16])
        peak, factors, sums = weigh(stats)
        factors = [f.astype(BF).astype(F32) for f in factors]
        total = functools.reduce(jnp.add, [f * s for f, s in zip(factors, sums)])
        rolled = [pltpu.roll(f, 64, 1) for f in factors]
        joined = [jnp.where(lane8 < 64, factors[2 * p], rolled[2 * p + 1]) for p in range(4)]
        new = jnp.where(lane8 < 64, peak, pltpu.roll(total, 64, 1))
        high = new.astype(BF).astype(F32)
        low = new - high
        for zl in range(4):
            z = halves[n] * 4 + zl
            value = jnp.zeros((16, 128), F32)
            for head in range(2):
                unit = 2 * zl + head
                mix = spread([x[unit : unit + 1] for x in joined], row, lane).astype(BF)
                at = base + unit * 64
                parts = in_ref[:, at : at + 64, :].reshape(512, 128)
                o_ref[z, head * 64 : head * 64 + 64, :] = dot_nn(mix, parts).astype(BF)
                value = jnp.where(tile == 2 * head, high[unit : unit + 1], value)
                value = jnp.where(tile == 2 * head + 1, low[unit : unit + 1], value)
            o_ref[z, 128:144, :] = value.astype(BF)
            pltpu.make_async_copy(o_ref.at[z], out_ref.at[z], sem.at[4 * n + zl]).start()
    for n in range(2):
        for zl in range(4):
            z = halves[n] * 4 + zl
            pltpu.make_async_copy(o_ref.at[z], out_ref.at[z], sem.at[4 * n + zl]).wait()


def fold(parts):
    return pl.pallas_call(
        fold_kernel,
        in_specs=[pl.BlockSpec(memory_space=pltpu.VMEM)],
        out_specs=pl.BlockSpec(memory_space=pl.ANY),
        out_shape=jax.ShapeDtypeStruct((8, 144, 128), BF),
        scratch_shapes=[pltpu.VMEM((8, 144, 128), BF), pltpu.SemaphoreType.DMA((8,))],
        compiler_params=pltpu.CompilerParams(vmem_limit_bytes=24 * MIB),
        name="fold",
    )(parts)


def prompt_kernel(where, slots, *refs):
    q_refs, kv_refs, o_ref, st_ref = refs[:8], refs[8:12], refs[12], refs[13]
    row, lane = eye_mask(64)
    query = where[1] * 4 + lax.broadcasted_iota(jnp.int32, (64, 64), 0) // 16
    column = lax.broadcasted_iota(jnp.int32, (64, 64), 1)
    mine = where[1] // 16
    for h in range(2):
        q = q_refs[4 * h][...]
        for j in range(1, 4):
            q = jnp.where(slots[j] == mine, q_refs[4 * h + j][...], q)
        scores = []
        for j in range(4):
            part = dot_nt(q, kv_refs[j][h * 128 : h * 128 + 64, :]) * SCALE
            seen = column + slots[j] * 64 <= query
            scores.append(jnp.where(seen, part, -jnp.inf))
        top = functools.reduce(jnp.maximum, [jnp.max(s, axis=1, keepdims=True) for s in scores])
        top = jnp.ceil(top)
        acc = jnp.zeros((64, 128), F32)
        total = jnp.zeros((64, 1), F32)
        for j in range(4):
            weights = jnp.exp2(scores[j] - top).astype(BF)
            total = total + jnp.sum(weights.astype(F32), axis=1, keepdims=True)
            acc = acc + dot_nn(weights, kv_refs[j][h * 128 + 64 : h * 128 + 128, :])
        o_ref[h] = acc.astype(BF)
        pair = jnp.where(lane == row, top, jnp.where(lane == row + 64, total, 0.0))
        st_ref[h] = jnp.broadcast_to(jnp.sum(pair, axis=0, keepdims=True), (8, 128))


def prompt_part(qs, where, slots):
    first = pl.BlockSpec((64, 128), lambda i, w, s: (w[0], 0))
    second = pl.BlockSpec((64, 128), lambda i, w, s: (16 + w[0], 0))
    kv_spec = pl.BlockSpec((256, 128), lambda i, w, s: (8, 0))
    return pl.pallas_call(
        prompt_kernel,
        grid_spec=pltpu.PrefetchScalarGridSpec(
            num_scalar_prefetch=2,
            grid=(1,),
            in_specs=[first] * 4 + [second] * 4 + [kv_spec] * 4,
            out_specs=[
                pl.BlockSpec((2, 64, 128), lambda i, w, s: (0, 0, 0)),
                pl.BlockSpec((2, 8, 128), lambda i, w, s: (0, 0, 0)),
            ],
        ),
        out_shape=[
            jax.ShapeDtypeStruct((2, 64, 128), BF),
            jax.ShapeDtypeStruct((2, 8, 128), F32),
        ],
        compiler_params=pltpu.CompilerParams(vmem_limit_bytes=40 * MIB),
        name="prompt",
    )(where, slots, *qs, *qs, *qs)


def final_kernel(got_ref, po_ref, pst_ref, o_ref):
    row, lane = eye_mask(64)
    for h in range(2):
        stats = []
        for src in range(8):
            block = got_ref[src, 128:144, :].astype(F32)
            stats.append(block[2 * h : 2 * h + 1] + block[2 * h + 1 : 2 * h + 2])
        stats.append(pst_ref[h][0:1])
        peak, factors, sums = weigh(stats)
        total = functools.reduce(jnp.add, [f * s for f, s in zip(factors, sums)])
        inverse = 1.0 / jnp.where(lane[0:1] < 64, total, 1.0)
        factors = [f * inverse for f in factors]
        factors.append(jnp.zeros_like(inverse))
        mix = spread([pair_up(factors[2 * p], factors[2 * p + 1], lane) for p in range(5)], row, lane)
        parts = got_ref[:, h * 64 : h * 64 + 64, :].reshape(512, 128)
        parts = jnp.concatenate([parts, po_ref[h], jnp.zeros((64, 128), BF)], axis=0)
        high = mix.astype(BF)
        low = (mix - high.astype(F32)).astype(BF)
        out = dot_nn(high, parts) + dot_nn(low, parts)
        o_ref[:, h * 16 : h * 16 + 16, :] = out.astype(BF).reshape(4, 16, 128)


def final(got, part_out, part_stats):
    return pl.pallas_call(
        final_kernel,
        out_shape=jax.ShapeDtypeStruct((4, 32, 128), BF),
        compiler_params=pltpu.CompilerParams(vmem_limit_bytes=16 * MIB),
        name="final",
    )(got, part_out, part_stats)


def body(
    queries,
    prompt_keys,
    prompt_values,
    cache_keys,
    cache_values,
    cache_lengths,
    offset,
    prompt_positions,
):
    axes = ("context", "tensor")
    context = lax.axis_index("context").astype(jnp.int32)
    own, swapped, ahead, back = turn(queries, offset, prompt_positions, prompt_keys, prompt_values)
    ahead = lax.ppermute(ahead, axes, shift(1, 0))
    back = lax.ppermute(back, axes, shift(-1, 1))
    swapped = lax.ppermute(swapped, axes, shift(0, 1))
    keys, values = lay(cache_keys, cache_values, cache_lengths)

    plane = [[z * 8 + r for r in range(8)] for z in range(8)]
    column = [[z * 8 + r for z in range(8)] for r in range(8)]

    def swap(parts, groups):
        return lax.all_to_all(
            parts, "context", split_axis=0, concat_axis=0, axis_index_groups=groups, tiled=True
        )

    parts = attend((own, swapped), keys, values, None, "near")
    parts = attend((ahead, back), keys, values, parts, "far")
    parts = swap(parts, plane)
    where = jnp.stack([context % 16, context])
    slots = jnp.stack(slots_of())
    part_out, part_stats = prompt_part((own, swapped, ahead, back), where, slots)
    got = swap(fold(parts), column)
    return final(got, part_out, part_stats)


def solution(mesh):
    in_specs = (
        P("tensor", None, None),
        P("tensor", None, None),
        P("tensor", None, None),
        P("context", "tensor", None),
        P("context", "tensor", None),
        P("context"),
        P(),
        P("tensor"),
    )
    out_specs = P("context", "tensor", None)
    return jax.shard_map(body, mesh=mesh, in_specs=in_specs, out_specs=out_specs, check_vma=False)
```

```python
import functools
import math

import jax
import jax.numpy as jnp
import numpy as np
from jax import lax
from jax.experimental import pallas as pl
from jax.experimental.pallas import tpu as pltpu
from jax.sharding import PartitionSpec as P

SCALE = math.log2(math.e) / math.sqrt(128.0)
BF = jnp.bfloat16
F32 = jnp.float32
MIB = 2**20
BIG = 60 * MIB
KEY_BLOCK = 512
SUB = 256


def linear(z, x, y, core):
    y = y % 4
    return ((z % 8) * 8 + (x % 4) * 2 + y // 2) * 4 + (y % 2) * 2 + core % 2


def shift(dy, dcore):
    return [
        (linear(z, x, y, k), linear(z, x, y + dy, k + dcore))
        for z in range(8)
        for x in range(4)
        for y in range(4)
        for k in range(2)
    ]


def dot_nt(a, b):
    return lax.dot_general(a, b, (((1,), (1,)), ((), ())), preferred_element_type=F32)


def dot_nn(a, b):
    return jnp.dot(a, b, preferred_element_type=F32)


def slots_of():
    tensor = lax.axis_index("tensor").astype(jnp.int32)
    core = lax.rem(tensor, 2)
    other = 2 * (1 - lax.div(tensor, 2))
    return tensor, tensor + 1 - 2 * core, other + core, other + 1 - core


def turn_kernel(offset, pos_ref, freq_ref, k_ref, v_ref, q_ref, *refs):
    outs, (q_s, out_s, cos_s, sin_s, wide_s, in_sem, out_sem) = refs[:4], refs[4:]
    slots = slots_of()

    def fetch(j):
        heads = pl.ds(pl.multiple_of(slots[j] * 32, 32), 32)
        return pltpu.make_async_copy(q_ref.at[:, heads, :], q_s.at[j], in_sem.at[j])

    def send(j):
        return pltpu.make_async_copy(out_s.at[j], outs[j], out_sem.at[j])

    order = (2, 3, 1, 0)
    for j in order:
        fetch(j).start()
    row = lax.broadcasted_iota(jnp.int32, (64, 64), 0)
    column = lax.broadcasted_iota(jnp.int32, (64, 64), 1)
    position = (pos_ref[...] + offset[0]).astype(F32)
    position = jnp.sum(jnp.where(row == column, position, 0.0), axis=1, keepdims=True)
    left = lax.broadcasted_iota(jnp.int32, (32, 128), 1) < 64
    angle = jnp.where(left, position[0:32], position[32:64]) * freq_ref[...]
    both = []
    for value in (jnp.cos(angle), jnp.sin(angle)):
        moved = pltpu.roll(value, 64, 1)
        above = jnp.where(left, value, moved)
        below = jnp.where(left, moved, value)
        both.append(jnp.concatenate([above, below], axis=0))
    lane = lax.broadcasted_iota(jnp.int32, (64, 128), 1)
    cosine = both[0]
    sine = jnp.where(lane < 64, -both[1], both[1])
    cos_s[...] = cosine
    sin_s[...] = sine
    wide = k_ref[...].astype(F32)
    rolled = pltpu.roll(wide.reshape(512, 128), 64, 1).reshape(64, 8, 128)
    wide_s[0] = (wide * cosine[:, None, :] + rolled * sine[:, None, :]).reshape(512, 128)
    wide_s[1] = v_ref[...].astype(F32).reshape(512, 128)
    for j in order:
        fetch(j).wait()

        @pl.loop(0, 4, unroll=True)
        def _(i):
            rows = pl.ds(pl.multiple_of(i * 16, 16), 16)
            cosine = cos_s[rows, :][:, None, :]
            sine = sin_s[rows, :][:, None, :]
            for head in range(2):
                wide = q_s[j, rows, head * 16 : head * 16 + 16, :].astype(F32)
                rolled = pltpu.roll(wide.reshape(256, 128), 64, 1).reshape(16, 16, 128)
                value = (wide * cosine + rolled * sine).reshape(256, 128).astype(BF)
                out_s[j, pl.ds(pl.multiple_of(head * 1024 + i * 256, 256), 256), :] = value

        for head in range(2):
            for n in range(2):
                start = 2048 + head * 128 + n * 64
                picked = wide_s[n, pl.ds(2 * slots[j] + head, 64, 8), :]
                out_s[j, start : start + 64, :] = picked.astype(BF)
        send(j).start()
    for j in order:
        send(j).wait()


def turn(queries, offset, positions, keys, values):
    freq = np.exp(np.arange(64, dtype=np.float32) * np.float32(-2.0 * math.log(500000.0) / 128))
    freq = jnp.asarray(np.concatenate([freq, freq])[None, :], F32)
    vmem = pl.BlockSpec(memory_space=pltpu.VMEM)
    hbm = pl.BlockSpec(memory_space=pl.ANY)
    return pl.pallas_call(
        turn_kernel,
        in_specs=[pl.BlockSpec(memory_space=pltpu.SMEM)] + [vmem] * 4 + [hbm],
        out_specs=[hbm] * 4,
        out_shape=[jax.ShapeDtypeStruct((2304, 128), BF)] * 4,
        scratch_shapes=[
            pltpu.VMEM((4, 64, 32, 128), BF),
            pltpu.VMEM((4, 2304, 128), BF),
            pltpu.VMEM((64, 128), F32),
            pltpu.VMEM((64, 128), F32),
            pltpu.VMEM((2, 512, 128), F32),
            pltpu.SemaphoreType.DMA((4,)),
            pltpu.SemaphoreType.DMA((4,)),
        ],
        compiler_params=pltpu.CompilerParams(vmem_limit_bytes=BIG),
        name="turn",
    )(offset, positions.reshape(1, 64), freq, keys, values, queries)


def lay_kernel(length, k_ref, v_ref, ko_ref, vo_ref, wide_s):
    for c in range(4):
        live = lax.broadcasted_iota(jnp.int32, (512, 128), 0) + c * 512 < length[0]
        rows = slice(c * 512, c * 512 + 512)
        wide_s[0] = k_ref[c * 1024 : c * 1024 + 1024, :].astype(F32)
        wide_s[1] = v_ref[c * 1024 : c * 1024 + 1024, :].astype(F32)
        first = k_ref[0:16, :].astype(F32)
        one = jnp.where(live, 1.0, 0.0).astype(BF)
        for head in range(2):
            keys = wide_s[0, pl.ds(head, 512, 2), :]
            values = wide_s[1, pl.ds(head, 512, 2), :]
            ko_ref[head, rows, :] = jnp.where(live, keys, first[head : head + 1, :]).astype(BF)
            vo_ref[head, rows, 0:128] = jnp.where(live, values, 0.0).astype(BF)
            vo_ref[head, rows, 128:256] = one


def lay(keys, values, length):
    vmem = pl.BlockSpec(memory_space=pltpu.VMEM)
    return pl.pallas_call(
        lay_kernel,
        in_specs=[pl.BlockSpec(memory_space=pltpu.SMEM), vmem, vmem],
        out_specs=[vmem, vmem],
        out_shape=[
            jax.ShapeDtypeStruct((2, 2048, 128), BF),
            jax.ShapeDtypeStruct((2, 2048, 256), BF),
        ],
        scratch_shapes=[pltpu.VMEM((2, 1024, 128), F32)],
        compiler_params=pltpu.CompilerParams(vmem_limit_bytes=24 * MIB),
        name="lay",
    )(length, keys.reshape(4096, 128), values.reshape(4096, 128))


def eye_mask(rows):
    row = lax.broadcasted_iota(jnp.int32, (rows, 128), 0)
    lane = lax.broadcasted_iota(jnp.int32, (rows, 128), 1)
    return row, lane


def attend_kernel(q0, q1, k_ref, v_ref, *refs, base):
    o_ref, q_s, o_s, st_s, o_sem, st_sem = refs[-6:]
    core = lax.rem(lax.axis_index("tensor").astype(jnp.int32), 2)

    def place(j):
        return 2 * (core + j * (1 - 2 * core))

    def send(head, j, half):
        start = pl.multiple_of((2 * (place(j) + half) + head) * 64, 64)
        return pltpu.make_async_copy(
            o_s.at[:, pl.ds(start, 64), :],
            o_ref.at[:, pl.ds(pl.multiple_of(base + start, 16), 64), :],
            o_sem.at[2 * head + j, half],
        )

    row, lane = eye_mask(64)

    @pl.loop(0, 2)
    def _(head):
        for j in range(2):
            for s in range(4):
                rows = pl.ds(pl.multiple_of(head * 1024 + s * SUB, SUB), SUB)
                q = (q0, q1)[j][rows, :]
                peak = None
                for b in range(2048 // KEY_BLOCK):
                    keys = slice(b * KEY_BLOCK, (b + 1) * KEY_BLOCK)
                    scores = dot_nt(q, k_ref[head, keys, :])
                    top = jnp.ceil(jnp.max(scores, axis=1, keepdims=True) * SCALE)
                    new = top if peak is None else jnp.maximum(peak, top)
                    weights = jnp.exp2(scores * SCALE - new).astype(BF)
                    part = dot_nn(weights, v_ref[head, keys, :])
                    acc = part if peak is None else acc * jnp.exp2(peak - new) + part
                    peak = new
                unit = 2 * (place(j) + s // 2) + head
                for d in range(4):
                    dest = 4 * (s % 2) + d
                    rows = slice(d * 64, (d + 1) * 64)
                    to = pl.ds(pl.multiple_of(unit * 64, 64), 64)
                    o_s[dest, to, :] = acc[rows, 0:128].astype(BF)
                    pair = jnp.where(
                        lane == row,
                        peak[rows, :],
                        jnp.where(lane == row + 64, acc[rows, 128:256], 0.0),
                    )
                    st_s[dest, pl.ds(unit, 1), :] = jnp.sum(pair, axis=0, keepdims=True)
            send(head, j, 0).start()
            send(head, j, 1).start()

    for dest in range(8):
        stats = st_s[dest]
        high = stats.astype(BF).astype(F32)
        o_s[dest, 512:528, :] = jnp.concatenate([high, stats - high], axis=0).astype(BF)
    tail = pltpu.make_async_copy(
        o_s.at[:, pl.ds(512, 16), :], o_ref.at[:, pl.ds(base + 512, 16), :], st_sem
    )
    tail.start()
    for head in range(2):
        for j in range(2):
            for half in range(2):
                send(head, j, half).wait()
    tail.wait()


def attend(qs, keys, values, before, name):
    any_space = pl.BlockSpec(memory_space=pl.ANY)
    args = [*qs, keys, values]
    aliases = {}
    if before is not None:
        aliases = {len(args): 0}
        args.append(before)
    return pl.pallas_call(
        functools.partial(attend_kernel, base=0 if before is None else 528),
        in_specs=[pl.BlockSpec(memory_space=pltpu.VMEM)] * 4 + [any_space] * (len(args) - 4),
        out_specs=any_space,
        scratch_shapes=[
            pltpu.VMEM((1024, 128), BF),
            pltpu.VMEM((8, 528, 128), BF),
            pltpu.VMEM((8, 8, 128), F32),
            pltpu.SemaphoreType.DMA((4, 2)),
            pltpu.SemaphoreType.DMA(()),
        ],
        out_shape=jax.ShapeDtypeStruct((8, 1056, 128), BF),
        input_output_aliases=aliases,
        compiler_params=pltpu.CompilerParams(vmem_limit_bytes=40 * MIB),
        cost_estimate=pl.CostEstimate(
            flops=4 * 4096 * 2048 * 128, bytes_accessed=4 * MIB, transcendentals=4096 * 2048
        ),
        name=name,
    )(*args)


def weigh(stats):
    peak = functools.reduce(jnp.maximum, stats)
    factors = [jnp.exp2(s - peak) for s in stats]
    sums = [pltpu.roll(s, 64, 1) for s in stats]
    return peak, factors, sums


def spread(pairs, row, lane):
    hit = (lane == row) | (lane == row + 64)
    return jnp.concatenate([jnp.where(hit, p, 0.0) for p in pairs], axis=1)


def pair_up(first, second, lane):
    return jnp.where(lane[0:1] < 64, first, pltpu.roll(second, 64, 1))


def fold_kernel(in_ref, out_ref, o_ref, sem):
    half = lax.div(lax.axis_index("tensor").astype(jnp.int32), 2)
    halves = (half, 1 - half)
    row, lane = eye_mask(64)
    lane8 = lax.broadcasted_iota(jnp.int32, (8, 128), 1)
    tile = lax.broadcasted_iota(jnp.int32, (16, 128), 0)
    for n in range(2):
        base = 528 * n
        stats = []
        for src in range(8):
            block = in_ref[src, base + 512 : base + 528, :].astype(F32)
            stats.append(block[0:8] + block[8:16])
        peak, factors, sums = weigh(stats)
        factors = [f.astype(BF).astype(F32) for f in factors]
        total = functools.reduce(jnp.add, [f * s for f, s in zip(factors, sums)])
        rolled = [pltpu.roll(f, 64, 1) for f in factors]
        joined = [jnp.where(lane8 < 64, factors[2 * p], rolled[2 * p + 1]) for p in range(4)]
        new = jnp.where(lane8 < 64, peak, pltpu.roll(total, 64, 1))
        high = new.astype(BF).astype(F32)
        low = new - high
        for zl in range(4):
            z = halves[n] * 4 + zl
            value = jnp.zeros((16, 128), F32)
            for head in range(2):
                unit = 2 * zl + head
                mix = spread([x[unit : unit + 1] for x in joined], row, lane).astype(BF)
                at = base + unit * 64
                parts = in_ref[:, at : at + 64, :].reshape(512, 128)
                o_ref[z, head * 64 : head * 64 + 64, :] = dot_nn(mix, parts).astype(BF)
                value = jnp.where(tile == 2 * head, high[unit : unit + 1], value)
                value = jnp.where(tile == 2 * head + 1, low[unit : unit + 1], value)
            o_ref[z, 128:144, :] = value.astype(BF)
            pltpu.make_async_copy(o_ref.at[z], out_ref.at[z], sem.at[4 * n + zl]).start()
    for n in range(2):
        for zl in range(4):
            z = halves[n] * 4 + zl
            pltpu.make_async_copy(o_ref.at[z], out_ref.at[z], sem.at[4 * n + zl]).wait()


def fold(parts):
    return pl.pallas_call(
        fold_kernel,
        in_specs=[pl.BlockSpec(memory_space=pltpu.VMEM)],
        out_specs=pl.BlockSpec(memory_space=pl.ANY),
        out_shape=jax.ShapeDtypeStruct((8, 144, 128), BF),
        scratch_shapes=[pltpu.VMEM((8, 144, 128), BF), pltpu.SemaphoreType.DMA((8,))],
        compiler_params=pltpu.CompilerParams(vmem_limit_bytes=24 * MIB),
        name="fold",
    )(parts)


def prompt_kernel(where, slots, *refs):
    q_refs, kv_refs, o_ref, st_ref = refs[:8], refs[8:12], refs[12], refs[13]
    row, lane = eye_mask(64)
    query = where[1] * 4 + lax.broadcasted_iota(jnp.int32, (64, 64), 0) // 16
    column = lax.broadcasted_iota(jnp.int32, (64, 64), 1)
    mine = where[1] // 16
    for h in range(2):
        q = q_refs[4 * h][...]
        for j in range(1, 4):
            q = jnp.where(slots[j] == mine, q_refs[4 * h + j][...], q)
        scores = []
        for j in range(4):
            part = dot_nt(q, kv_refs[j][h * 128 : h * 128 + 64, :]) * SCALE
            seen = column + slots[j] * 64 <= query
            scores.append(jnp.where(seen, part, -jnp.inf))
        top = functools.reduce(jnp.maximum, [jnp.max(s, axis=1, keepdims=True) for s in scores])
        top = jnp.ceil(top)
        acc = jnp.zeros((64, 128), F32)
        total = jnp.zeros((64, 1), F32)
        for j in range(4):
            weights = jnp.exp2(scores[j] - top).astype(BF)
            total = total + jnp.sum(weights.astype(F32), axis=1, keepdims=True)
            acc = acc + dot_nn(weights, kv_refs[j][h * 128 + 64 : h * 128 + 128, :])
        o_ref[h] = acc.astype(BF)
        pair = jnp.where(lane == row, top, jnp.where(lane == row + 64, total, 0.0))
        st_ref[h] = jnp.broadcast_to(jnp.sum(pair, axis=0, keepdims=True), (8, 128))


def prompt_part(qs, where, slots):
    first = pl.BlockSpec((64, 128), lambda i, w, s: (w[0], 0))
    second = pl.BlockSpec((64, 128), lambda i, w, s: (16 + w[0], 0))
    kv_spec = pl.BlockSpec((256, 128), lambda i, w, s: (8, 0))
    return pl.pallas_call(
        prompt_kernel,
        grid_spec=pltpu.PrefetchScalarGridSpec(
            num_scalar_prefetch=2,
            grid=(1,),
            in_specs=[first] * 4 + [second] * 4 + [kv_spec] * 4,
            out_specs=[
                pl.BlockSpec((2, 64, 128), lambda i, w, s: (0, 0, 0)),
                pl.BlockSpec((2, 8, 128), lambda i, w, s: (0, 0, 0)),
            ],
        ),
        out_shape=[
            jax.ShapeDtypeStruct((2, 64, 128), BF),
            jax.ShapeDtypeStruct((2, 8, 128), F32),
        ],
        compiler_params=pltpu.CompilerParams(vmem_limit_bytes=40 * MIB),
        name="prompt",
    )(where, slots, *qs, *qs, *qs)


def final_kernel(got_ref, po_ref, pst_ref, o_ref):
    row, lane = eye_mask(64)
    for h in range(2):
        stats = []
        for src in range(8):
            block = got_ref[src, 128:144, :].astype(F32)
            stats.append(block[2 * h : 2 * h + 1] + block[2 * h + 1 : 2 * h + 2])
        stats.append(pst_ref[h][0:1])
        peak, factors, sums = weigh(stats)
        total = functools.reduce(jnp.add, [f * s for f, s in zip(factors, sums)])
        inverse = 1.0 / jnp.where(lane[0:1] < 64, total, 1.0)
        factors = [f * inverse for f in factors]
        factors.append(jnp.zeros_like(inverse))
        mix = spread([pair_up(factors[2 * p], factors[2 * p + 1], lane) for p in range(5)], row, lane)
        parts = got_ref[:, h * 64 : h * 64 + 64, :].reshape(512, 128)
        parts = jnp.concatenate([parts, po_ref[h], jnp.zeros((64, 128), BF)], axis=0)
        high = mix.astype(BF)
        low = (mix - high.astype(F32)).astype(BF)
        out = dot_nn(high, parts) + dot_nn(low, parts)
        o_ref[:, h * 16 : h * 16 + 16, :] = out.astype(BF).reshape(4, 16, 128)


def final(got, part_out, part_stats):
    return pl.pallas_call(
        final_kernel,
        out_shape=jax.ShapeDtypeStruct((4, 32, 128), BF),
        compiler_params=pltpu.CompilerParams(vmem_limit_bytes=16 * MIB),
        name="final",
    )(got, part_out, part_stats)


def body(
    queries,
    prompt_keys,
    prompt_values,
    cache_keys,
    cache_values,
    cache_lengths,
    offset,
    prompt_positions,
):
    axes = ("context", "tensor")
    context = lax.axis_index("context").astype(jnp.int32)
    own, swapped, ahead, back = turn(queries, offset, prompt_positions, prompt_keys, prompt_values)
    ahead = lax.ppermute(ahead, axes, shift(1, 0))
    back = lax.ppermute(back, axes, shift(-1, 1))
    swapped = lax.ppermute(swapped, axes, shift(0, 1))
    keys, values = lay(cache_keys, cache_values, cache_lengths)

    plane = [[z * 8 + r for r in range(8)] for z in range(8)]
    column = [[z * 8 + r for z in range(8)] for r in range(8)]

    def swap(parts, groups):
        return lax.all_to_all(
            parts, "context", split_axis=0, concat_axis=0, axis_index_groups=groups, tiled=True
        )

    parts = attend((own, swapped), keys, values, None, "near")
    parts = attend((ahead, back), keys, values, parts, "far")
    parts = swap(parts, plane)
    where = jnp.stack([context % 16, context])
    slots = jnp.stack(slots_of())
    part_out, part_stats = prompt_part((own, swapped, ahead, back), where, slots)
    got = swap(fold(parts), column)
    return final(got, part_out, part_stats)


def solution(mesh):
    in_specs = (
        P("tensor", None, None),
        P("tensor", None, None),
        P("tensor", None, None),
        P("context", "tensor", None),
        P("context", "tensor", None),
        P("context"),
        P(),
        P("tensor"),
    )
    out_specs = P("context", "tensor", None)
    return jax.shard_map(body, mesh=mesh, in_specs=in_specs, out_specs=out_specs, check_vma=False)
```
